128 devices in a mesh: seq: 32 (over z, x, core), ret: 4 (over y).
Axes of the slice: x: 4, y: 4, z: 4, core: 2. Of those that a mesh axis runs over, the one named last changes fastest.
Arguments:
- activations: bfloat16 [16384, 4096], P('seq'), may hold values from -6 to 6
- grad_out: bfloat16 [16384, 4096], P('seq'), may hold values from -6 to 6
- database: bfloat16 [1024, 128, 896], P(('seq', 'ret')), may hold values from -6 to 6
- owners: int32 [256, 2], P('seq'), may hold values from 0 to 3, all different within a row; in each aligned block of 8 rows (0 to 7, 8 to 15, ...) at most 5 rows name the same one
- row_index: int32 [256, 2], P('seq'), may hold values from 0 to 7
- w_cond: bfloat16 [2, 4096, 896], P(None, 'seq', 'ret'), may hold values from -0.09375 to 0.09375
- w_enc: bfloat16 [2, 896, 896], replicated, may hold values from -0.1875 to 0.1875
- w_query: bfloat16 [4096, 2048], P('seq', 'ret'), may hold values from -0.09375 to 0.09375
- w_kv: bfloat16 [2, 896, 2048], P(None, 'seq', 'ret'), may hold values from -0.1875 to 0.1875
- w_out: bfloat16 [2048, 4096], P('ret', 'seq'), may hold values from -0.125 to 0.125
Outputs:
- grad_x: bfloat16 [16384, 4096], P('seq', 'ret')
- grad_db: bfloat16 [1024, 128, 896], P(('seq', 'ret'))
- grad_wq: bfloat16 [4096, 2048], P('seq', 'ret')
- grad_wcond: bfloat16 [2, 4096, 896], P(None, 'seq', 'ret')
The draws below stay inside these ranges and needn't reach their ends.
Inputs may be any that keep to these rules, and one draw needn't show every extreme that they name: The 2 neighbours of a stretch come from different owners. Among the 8 stretches of one index of seq, at most 5 neighbours come from one owner, and some index reaches 5.
All inputs are finite; a program needn't handle non-finite values.
Results may differ from the reference program's by a relative error of at most 0.035.
Values may be sent and summed in bfloat16 or wider, within the bound.
No kernel may reach another device: no remote copies, remote signals or barrier semaphores. Data moves between devices by JAX's collectives and lax.ppermute only.
A program may use at most 128 MiB of HBM per device.

```python
import math
import jax
import jax.numpy as jnp
import numpy as np
from jax import lax

D = 4096
HD = 128
E = 896
ENC_HD = 128
STRETCH = 64
NLEN = 128
NBR = 2
CH = 8
DB_ROWS = 8
OWNERS = 4
INNER = 2048
NCH = 256
TOKENS = 16384
DBT = 1024
MOST = 5


def with_ends(result, rng, least, largest):
    index_at = [jax.random.randint(jax.random.fold_in(rng, axis), (), 0, length) for axis, length in enumerate(result.shape)]
    widest = result.shape.index(max(result.shape))
    neighbour = index_at[:widest] + [(index_at[widest] + 1) % result.shape[widest]] + index_at[widest + 1:]
    return result.at[tuple(index_at)].set(least).at[tuple(neighbour)].set(largest)


def with_spikes(result, stream_key, source, target, blocks, factor):
    def block_of(position):
        return (jnp.arange(result.shape[position]) // (result.shape[position] // blocks)).reshape((-1,) + (1,) * (result.ndim - 1 - position))

    first = jax.random.permutation(stream_key, blocks)[block_of(target)]
    second = (block_of(target) + blocks // 2) % blocks
    return jnp.where((block_of(source) == first) | (block_of(source) == second), factor * result, result)


def levels(stream_key, shape, shards, smallest, largest):
    def one(axis_at, shards_of):
        heights = jax.random.uniform(jax.random.fold_in(jax.random.fold_in(stream_key, 6), axis_at), (shards_of,), jnp.float32, smallest / len(shards), largest / len(shards))
        return jnp.repeat(jnp.exp(heights), shape[axis_at] // shards_of).reshape((-1,) + (1,) * (len(shape) - axis_at - 1))

    gain = one(*shards[0])
    for cut in shards[1:]:
        gain = gain * one(*cut)
    return gain


def shared_out(rng, own, number, rows, number_of, top, most, lean):
    order = jax.random.permutation(rng, number_of)
    crowded, usual = load_shares(number_of, rows * top, most, lean, True), load_shares(number_of, rows * top, most, lean, False)
    places = jnp.arange(number_of)

    def named(sizes, rotation):
        used = int((sizes > 0).sum())
        fixed = max(1, used // 4)
        passed = fixed + (places - fixed + rotation * (used - fixed)) % max(1, number_of - fixed)
        return jnp.zeros((number_of,), jnp.int32).at[order[jnp.where(places < fixed, places, passed)]].set(jnp.asarray(sizes, jnp.int32))

    sizes = jnp.where(number % 4 == 0, named(crowded, number // 4), named(usual, number - number // 4 - 1))
    mixed = jax.random.permutation(jax.random.fold_in(own, 3), number_of)
    source_of, receiver = mixed[0:number_of // 2 * 2:2], mixed[1:number_of // 2 * 2:2]
    slack = jnp.minimum(sizes[source_of] - 1, most - sizes[receiver]) // 2
    slack = jnp.where((source_of == order[0]) | (receiver == order[0]) | (sizes[receiver] == 0), 0, jnp.maximum(slack, 0))
    passed = jax.random.randint(jax.random.fold_in(own, 4), (number_of // 2,), 0, 1 << 20) % (slack + 1)
    sizes = sizes.at[source_of].add(-passed).at[receiver].add(passed)
    labels = jnp.searchsorted(jnp.cumsum(sizes), jnp.arange(rows * top), side="right").astype(jnp.int32)
    grid = labels.reshape(top, rows).T
    grid = grid[jax.random.permutation(jax.random.fold_in(own, 1), rows)]
    rotation = jax.random.randint(jax.random.fold_in(own, 2), (rows, 1), 0, top)
    return jnp.take_along_axis(grid, (jnp.arange(top)[None, :] + rotation) % top, axis=1)


def load_shares(count, total, most, lean, full):
    weights = [(1 << 20) // math.isqrt(rank ** lean) + 1 for rank in range(1, count + 1)]
    largest = most if full else min(most, max(-(-total // count), total * weights[0] // sum(weights)))
    least = 1 if total - largest >= count - 1 else 0
    given, rest = [largest] + [least] * (count - 1), total - largest - least * (count - 1)
    while rest > 0:
        movable = [i for i in range(1, count) if given[i] < largest] or [i for i in range(1, count) if given[i] < most]
        whole, budget = sum([weights[i] for i in movable]), rest
        for i in movable:
            more = min(most - given[i], max(1, budget * weights[i] // whole), rest)
            given[i] = given[i] + more
            rest = rest - more
    return np.array(given)


def bell_draw(stream_key, shape, width, bound, shards=(), kind=jnp.bfloat16):
    values = width * jax.random.normal(stream_key, shape, jnp.float32)
    if shards:
        values = values * levels(stream_key, shape, shards, -0.22, 0.18)
    return jnp.clip(values, -bound, bound).astype(kind)


def heavy_noise(rng, extent, width, reach, cuts, heavy, kind=jnp.bfloat16):
    result = width * jax.random.normal(rng, extent, jnp.float32)
    if cuts:
        result = result * levels(rng, extent, cuts, -0.22, 0.18)
    return jnp.clip(with_spikes(result, jax.random.fold_in(rng, 3), *heavy), -reach, reach).astype(kind)


def setup_inputs(seed: int = 0) -> dict:
    seeds = jax.random.split(jax.random.key(seed), 11)
    activations = heavy_noise(seeds[0], (TOKENS, D), 1.0, 6.0, ((0, 32),), (0, 1, 32, 2.75))
    grad_out = bell_draw(seeds[1], (TOKENS, D), 1.0, 6.0, ((0, 32),))
    database = bell_draw(seeds[2], (DBT, NLEN, E), 1.0, 6.0, ((0, 128),))
    owners_keys = jax.random.split(jax.random.fold_in(seeds[3], 1), NCH // CH)
    owners_turns = jax.random.permutation(jax.random.fold_in(seeds[3], 3), NCH // CH)
    owners = jax.vmap(lambda own, number: shared_out(jax.random.fold_in(seeds[3], 2), own, number, CH, OWNERS, NBR, MOST, 2))(owners_keys, owners_turns).reshape((NCH, NBR))
    row_index = with_ends(jax.random.randint(seeds[4], (NCH, NBR), 0, DB_ROWS), jax.random.fold_in(seeds[4], 1), 0, DB_ROWS - 1).astype(jnp.int32)
    w_cond = bell_draw(seeds[5], (2, D, E), D ** -0.5, 0.09375, ((1, 32), (2, 4)))
    w_enc = bell_draw(seeds[6], (2, E, E), E ** -0.5, 0.1875)
    w_query = bell_draw(seeds[7], (D, INNER), D ** -0.5, 0.09375, ((0, 32), (1, 4)))
    w_kv = bell_draw(seeds[8], (2, E, INNER), E ** -0.5, 0.1875, ((1, 32), (2, 4)))
    w_out = bell_draw(seeds[9], (INNER, D), INNER ** -0.5, 0.125, ((0, 4), (1, 32)))
    return dict(activations=activations, grad_out=grad_out, database=database, owners=owners, row_index=row_index, w_cond=w_cond, w_enc=w_enc, w_query=w_query, w_kv=w_kv, w_out=w_out)


def widen(array_low):
    return lax.optimization_barrier(array_low).astype(jnp.float32)


def flat_dot(left_op, right_op):
    leading = left_op.shape[:-1]
    product = jnp.dot(left_op.reshape(-1, left_op.shape[-1]), right_op, preferred_element_type=jnp.float32)
    return product.reshape(leading + (right_op.shape[1],))


def encode_rows(neighbour_rows, cond_pairs, w_enc):
    item_count, row_length, enc_width = neighbour_rows.shape
    head_count = enc_width // ENC_HD
    score_scale = ENC_HD ** -0.5
    enc_queries = flat_dot(neighbour_rows, w_enc[0]).astype(jnp.bfloat16)
    q_heads = widen(enc_queries).reshape(item_count, row_length, head_count, ENC_HD)
    k_heads = widen(cond_pairs[:, :, 0]).reshape(item_count, -1, head_count, ENC_HD)
    v_heads = widen(cond_pairs[:, :, 1]).reshape(item_count, -1, head_count, ENC_HD)
    scores = jnp.einsum("nthd,nshd->nhts", q_heads, k_heads) * score_scale
    exponent = jnp.exp(scores)
    attn_probs = exponent / jnp.sum(exponent, axis=-1, keepdims=True)
    probs_low = widen(attn_probs.astype(jnp.bfloat16))
    mixture = jnp.einsum("nhts,nshd->nthd", probs_low, v_heads).reshape(item_count, row_length, enc_width).astype(jnp.bfloat16)
    encoded = (neighbour_rows.astype(jnp.float32) + flat_dot(mixture, w_enc[1])).astype(jnp.bfloat16)
    return encoded, (q_heads, k_heads, v_heads, attn_probs, probs_low)


def encode_back(grad_encoded, w_enc, stored):
    q_heads, k_heads, v_heads, attn_probs, probs_low = stored
    item_count, row_length, enc_width = grad_encoded.shape
    head_count = enc_width // ENC_HD
    score_scale = ENC_HD ** -0.5
    grad_mixture = flat_dot(grad_encoded, w_enc[1].T).astype(jnp.bfloat16)
    g_heads = widen(grad_mixture).reshape(item_count, row_length, head_count, ENC_HD)
    grad_probs = jnp.einsum("nthd,nshd->nhts", g_heads, v_heads)
    centred = grad_probs - jnp.sum(attn_probs * grad_probs, axis=-1, keepdims=True)
    grad_scores = widen((attn_probs * centred * score_scale).astype(jnp.bfloat16))
    grad_queries = jnp.einsum("nhts,nshd->nthd", grad_scores, k_heads).reshape(item_count, row_length, enc_width).astype(jnp.bfloat16)
    grad_keys = jnp.einsum("nhts,nthd->nshd", grad_scores, q_heads).reshape(item_count, -1, enc_width)
    grad_values = jnp.einsum("nhts,nthd->nshd", probs_low, g_heads).reshape(item_count, -1, enc_width)
    grad_rows = grad_encoded.astype(jnp.float32) + flat_dot(grad_queries, w_enc[0].T)
    return grad_rows, jnp.stack([grad_keys, grad_values], axis=2)


def cross_attend(queries, prev_keys, prev_values, grad_att):
    stretch_count, stretch_len, inner_width = queries.shape
    head_count = inner_width // HD
    score_scale = HD ** -0.5
    q_heads = widen(queries).reshape(stretch_count, stretch_len, head_count, HD)
    k_heads = widen(prev_keys).reshape(stretch_count, -1, head_count, HD)
    v_heads = widen(prev_values).reshape(stretch_count, -1, head_count, HD)
    g_heads = widen(grad_att).reshape(stretch_count, stretch_len, head_count, HD)
    scores = jnp.einsum("cqhd,ckhd->chqk", q_heads, k_heads) * score_scale
    exponent = jnp.exp(scores)
    attn_probs = exponent / jnp.sum(exponent, axis=-1, keepdims=True)
    probs_low = widen(attn_probs.astype(jnp.bfloat16))
    grad_probs = jnp.einsum("cqhd,ckhd->chqk", g_heads, v_heads)
    centred = grad_probs - jnp.sum(attn_probs * grad_probs, axis=-1, keepdims=True)
    grad_scores = widen((attn_probs * centred * score_scale).astype(jnp.bfloat16))
    grad_q = jnp.einsum("chqk,ckhd->cqhd", grad_scores, k_heads).reshape(stretch_count, stretch_len, inner_width).astype(jnp.bfloat16)
    grad_k = jnp.einsum("chqk,cqhd->ckhd", grad_scores, q_heads).reshape(stretch_count, -1, inner_width).astype(jnp.bfloat16)
    grad_v = jnp.einsum("chqk,cqhd->ckhd", probs_low, g_heads).reshape(stretch_count, -1, inner_width).astype(jnp.bfloat16)
    return grad_q, grad_k, grad_v


def reference(activations, grad_out, database, owners, row_index, w_cond, w_enc, w_query, w_kv, w_out):
    stretch_total, pair_count = owners.shape
    token_count, model_width = activations.shape
    inner_width = w_query.shape[1]
    span = pair_count * NLEN
    block_of = (jnp.arange(stretch_total, dtype=jnp.int32) // CH)[:, None]
    global_row = ((block_of * OWNERS + owners) * DB_ROWS + row_index).reshape(-1).astype(jnp.int32)
    neighbour_rows = jnp.take(database, global_row, axis=0)
    cond_keys = flat_dot(activations, w_cond[0]).astype(jnp.bfloat16)
    cond_values = flat_dot(activations, w_cond[1]).astype(jnp.bfloat16)
    cond_stretches = jnp.stack([cond_keys, cond_values], axis=1).reshape(stretch_total, STRETCH, 2, E)
    entry_stretch = jnp.arange(stretch_total * pair_count, dtype=jnp.int32) // pair_count
    cond_entries = jnp.take(cond_stretches, entry_stretch, axis=0)
    encoded, stored = encode_rows(neighbour_rows, cond_entries, w_enc)
    key_rows = flat_dot(encoded, w_kv[0]).astype(jnp.bfloat16).reshape(stretch_total, span, inner_width)
    value_rows = flat_dot(encoded, w_kv[1]).astype(jnp.bfloat16).reshape(stretch_total, span, inner_width)
    empty = jnp.zeros((1, span, inner_width), jnp.bfloat16)
    prev_keys = jnp.concatenate([empty, key_rows[:-1]], axis=0)
    prev_values = jnp.concatenate([empty, value_rows[:-1]], axis=0)
    queries = flat_dot(activations, w_query).astype(jnp.bfloat16).reshape(stretch_total, STRETCH, inner_width)
    grad_att = flat_dot(grad_out, w_out.T).astype(jnp.bfloat16).reshape(stretch_total, STRETCH, inner_width)
    block_count = stretch_total // CH

    def per_block(pieces):
        return cross_attend(pieces[0], pieces[1], pieces[2], pieces[3])

    grad_q, grad_k, grad_v = lax.map(per_block, (
        queries.reshape(block_count, CH, STRETCH, inner_width),
        prev_keys.reshape(block_count, CH, span, inner_width),
        prev_values.reshape(block_count, CH, span, inner_width),
        grad_att.reshape(block_count, CH, STRETCH, inner_width)))
    grad_q = grad_q.reshape(token_count, inner_width)
    grad_k = grad_k.reshape(stretch_total, span, inner_width)
    grad_v = grad_v.reshape(stretch_total, span, inner_width)
    own_keys = jnp.concatenate([grad_k[1:], empty], axis=0).reshape(stretch_total * pair_count, NLEN, inner_width)
    own_values = jnp.concatenate([grad_v[1:], empty], axis=0).reshape(stretch_total * pair_count, NLEN, inner_width)
    group_width = inner_width // OWNERS
    grad_sum = jnp.zeros(neighbour_rows.shape, jnp.float32)
    for head_group in range(OWNERS):
        first_col = head_group * group_width
        group_term = flat_dot(own_keys[..., first_col:first_col + group_width], w_kv[0][:, first_col:first_col + group_width].T)
        group_term = group_term + flat_dot(own_values[..., first_col:first_col + group_width], w_kv[1][:, first_col:first_col + group_width].T)
        grad_sum = grad_sum + widen(group_term.astype(jnp.bfloat16))
    grad_encoded = grad_sum.astype(jnp.bfloat16)
    grad_rows, grad_cond = encode_back(grad_encoded, w_enc, stored)
    grad_db = jnp.zeros(database.shape, jnp.float32).at[global_row].add(grad_rows).astype(jnp.bfloat16)
    cond_total = grad_cond.reshape(stretch_total, pair_count, STRETCH, 2, E).sum(axis=1).reshape(token_count, 2, E).astype(jnp.bfloat16)
    grad_x = flat_dot(grad_q, w_query.T)
    grad_x = grad_x + flat_dot(cond_total[:, 0], w_cond[0].T) + flat_dot(cond_total[:, 1], w_cond[1].T)
    grad_x = grad_x.astype(jnp.bfloat16)

    def add_block(running, pieces):
        token_block, grad_block = pieces
        block_term = jnp.dot(token_block.T, grad_block, preferred_element_type=jnp.float32)
        return running + widen(block_term.astype(jnp.bfloat16)), None

    running, unused = lax.scan(add_block, jnp.zeros((model_width, inner_width), jnp.float32), (
        activations.reshape(block_count, CH * STRETCH, model_width),
        grad_q.reshape(block_count, CH * STRETCH, inner_width)))
    cond_running, unused_cond = lax.scan(add_block, jnp.zeros((model_width, 2 * E), jnp.float32), (
        activations.reshape(block_count, CH * STRETCH, model_width),
        cond_total.reshape(block_count, CH * STRETCH, 2 * E)))
    grad_wcond = cond_running.reshape(model_width, 2, E).transpose(1, 0, 2).astype(jnp.bfloat16)
    return grad_x, grad_db, running.astype(jnp.bfloat16), grad_wcond
```

```python
import functools

import jax
import jax.numpy as jnp
from jax import lax
from jax.experimental import pallas as pl
from jax.experimental.pallas import tpu as pltpu
from jax.sharding import PartitionSpec as P

HD = 128
BF = jnp.bfloat16
F32 = jnp.float32
VMEM_LIMIT = 40 * 1024 * 1024


def along_seq(value, steps):
    count = lax.axis_size("seq")
    first, last = (max(0, -steps), min(count, count - steps))
    return lax.ppermute(value, "seq", [(i, i + steps) for i in range(first, last)])


def around_ret(value, steps):
    count = lax.axis_size("ret")
    return lax.ppermute(value, "ret", [(i, (i + steps) % count) for i in range(count)])


def mm(left, right, contract):
    return lax.dot_general(left, right, (contract, ((), ())), preferred_element_type=F32)


NN = ((1,), (0,))
NT = ((1,), (1,))
TN = ((0,), (0,))


def cost(flops, nbytes):
    return pl.CostEstimate(flops=int(flops), bytes_accessed=int(nbytes), transcendentals=0)


def projections_kernel(x_ref, g_ref, w_ref, o_ref, acc_q, acc_g):
    step = pl.program_id(0)
    shards, rows, width = w_ref.shape
    half = width // 2

    @pl.when(step == 0)
    def _():
        acc_q[...] = jnp.zeros_like(acc_q)
        acc_g[...] = jnp.zeros_like(acc_g)

    w = w_ref[...].reshape(shards * rows, width)
    acc_q[...] += mm(x_ref[...], w[:, :half], NN)
    acc_g[...] += mm(g_ref[...], w[:, half:], NN)

    @pl.when(step == pl.num_programs(0) - 1)
    def _():
        o_ref[:, :half] = acc_q[...].astype(BF)
        o_ref[:, half:] = acc_g[...].astype(BF)


def projections(activations, grad_out, gathered, rows):
    tokens, model = activations.shape
    shards, _, width = gathered.shape
    per_step = 4
    depth = per_step * rows
    return pl.pallas_call(
        projections_kernel,
        grid=(shards // per_step,),
        in_specs=[
            pl.BlockSpec((tokens, depth), lambda i: (0, i)),
            pl.BlockSpec((tokens, depth), lambda i: (0, i)),
            pl.BlockSpec((per_step, rows, width), lambda i: (i, 0, 0)),
        ],
        out_specs=pl.BlockSpec((tokens, width), lambda i: (0, 0)),
        out_shape=jax.ShapeDtypeStruct((tokens, width), BF),
        scratch_shapes=[pltpu.VMEM((tokens, width // 2), F32)] * 2,
        compiler_params=pltpu.CompilerParams(vmem_limit_bytes=VMEM_LIMIT),
        cost_estimate=cost(
            2 * tokens * model * width, 2 * (2 * tokens * model + model * width + tokens * width)
        ),
        name="projections",
    )(activations, grad_out, gathered)


def encode_kernel(keep_ref, rows_ref, q_ref, k_ref, v_ref, w_ref, o_ref, mixed):
    enc_width = rows_ref.shape[-1]
    scale = HD ** (-0.5)
    keep = keep_ref[pl.program_id(0)]
    for h in range(enc_width // HD):
        cols = slice(h * HD, (h + 1) * HD)
        scores = mm(q_ref[0, :, cols], k_ref[:, cols], NT) * scale
        exponent = jnp.exp(scores)
        probs = exponent / jnp.sum(exponent, axis=-1, keepdims=True)
        mixed[:, cols] = mm(probs.astype(BF), v_ref[:, cols], NN).astype(BF)
    coded = rows_ref[0].astype(F32) + mm(mixed[...], w_ref[...], NN)
    o_ref[0] = jnp.where(keep > 0, coded, 0.0).astype(BF)


def encode(keep, rows, queries, keys, values, w_back, pair_count):
    entries, length, width = rows.shape
    stretch_len = keys.shape[0] // (entries // pair_count)
    one = pl.BlockSpec((1, length, width), lambda e, keep: (e, 0, 0))
    side = pl.BlockSpec((stretch_len, width), lambda e, keep: (e // pair_count, 0))
    return pl.pallas_call(
        encode_kernel,
        grid_spec=pltpu.PrefetchScalarGridSpec(
            num_scalar_prefetch=1,
            grid=(entries,),
            in_specs=[one, one, side, side, pl.BlockSpec((width, width), lambda e, keep: (0, 0))],
            out_specs=one,
            scratch_shapes=[pltpu.VMEM((length, width), BF)],
        ),
        out_shape=jax.ShapeDtypeStruct(rows.shape, BF),
        compiler_params=pltpu.CompilerParams(vmem_limit_bytes=VMEM_LIMIT),
        cost_estimate=cost(
            2 * entries * length * width * (width + 2 * stretch_len),
            2 * (3 * entries * length * width + width * width),
        ),
        name="encode",
    )(keep, rows, queries, keys, values, w_back)


def encode_back_kernel(
    keep_ref, t0, t1, t2, t3, q_ref, k_ref, v_ref, w_in_ref, w_back_ref,
    rows_out, keys_out, values_out, mixed, enc_q, acc_k, acc_v, *, pair_count,
):
    step = pl.program_id(0)
    enc_width = q_ref.shape[-1]
    scale = HD ** (-0.5)
    keep = keep_ref[step]
    total = (t0[0].astype(F32) + t1[0].astype(F32)) + (t2[0].astype(F32) + t3[0].astype(F32))
    coded = jnp.where(keep > 0, total, 0.0).astype(BF)
    mixed[...] = mm(coded, w_back_ref[...], NT).astype(BF)

    @pl.when(step % pair_count == 0)
    def _():
        acc_k[...] = jnp.zeros_like(acc_k)
        acc_v[...] = jnp.zeros_like(acc_v)

    for h in range(enc_width // HD):
        cols = slice(h * HD, (h + 1) * HD)
        q, k, v, g = q_ref[0, :, cols], k_ref[:, cols], v_ref[:, cols], mixed[:, cols]
        exponent = jnp.exp(mm(q, k, NT) * scale)
        probs = exponent / jnp.sum(exponent, axis=-1, keepdims=True)
        grad_probs = mm(g, v, NT)
        centred = grad_probs - jnp.sum(probs * grad_probs, axis=-1, keepdims=True)
        grad_scores = (probs * centred * scale).astype(BF)
        enc_q[:, cols] = mm(grad_scores, k, NN).astype(BF)
        acc_k[:, cols] += mm(grad_scores, q, TN)
        acc_v[:, cols] += mm(probs.astype(BF), g, TN)
    rows_out[0] = (coded.astype(F32) + mm(enc_q[...], w_in_ref[...], NT)).astype(BF)

    @pl.when(step % pair_count == pair_count - 1)
    def _():
        keys_out[...] = acc_k[...].astype(BF)
        values_out[...] = acc_v[...].astype(BF)


def encode_back(keep, terms, queries, keys, values, w_in, w_back, pair_count):
    entries, length, width = queries.shape
    stretch_len = keys.shape[0] // (entries // pair_count)
    one = pl.BlockSpec((1, length, width), lambda e, keep: (e, 0, 0))
    side = pl.BlockSpec((stretch_len, width), lambda e, keep: (e // pair_count, 0))
    whole = pl.BlockSpec((width, width), lambda e, keep: (0, 0))
    return pl.pallas_call(
        functools.partial(encode_back_kernel, pair_count=pair_count),
        grid_spec=pltpu.PrefetchScalarGridSpec(
            num_scalar_prefetch=1,
            grid=(entries,),
            in_specs=[one] * 5 + [side, side, whole, whole],
            out_specs=[one, side, side],
            scratch_shapes=[pltpu.VMEM((length, width), BF)] * 2
            + [pltpu.VMEM((stretch_len, width), F32)] * 2,
        ),
        out_shape=[
            jax.ShapeDtypeStruct(queries.shape, BF),
            jax.ShapeDtypeStruct(keys.shape, BF),
            jax.ShapeDtypeStruct(keys.shape, BF),
        ],
        compiler_params=pltpu.CompilerParams(vmem_limit_bytes=VMEM_LIMIT),
        cost_estimate=cost(
            4 * entries * length * width * (width + 3 * stretch_len),
            2 * (6 * entries * length * width + 2 * width * width),
        ),
        name="encode_back",
    )(keep, *terms, queries, keys, values, w_in, w_back)


def attend_kernel(place_ref, coded_ref, w_ref, qg_ref, *refs):
    term_out, grad_q_out, kv, grad_kv = refs[-4:]
    inner = qg_ref.shape[1] // 2
    scale = HD ** (-0.5)
    span = coded_ref.shape[0] * coded_ref.shape[1]
    coded = coded_ref[...].reshape(span, coded_ref.shape[2])
    kv[...] = mm(coded, w_ref[...], NN).astype(BF)
    for h in range(inner // HD):
        cols = slice(h * HD, (h + 1) * HD)
        right = slice(inner + h * HD, inner + (h + 1) * HD)
        q, g, k, v = qg_ref[:, cols], qg_ref[:, right], kv[:, cols], kv[:, right]
        exponent = jnp.exp(mm(q, k, NT) * scale)
        probs = exponent / jnp.sum(exponent, axis=-1, keepdims=True)
        grad_probs = mm(g, v, NT)
        centred = grad_probs - jnp.sum(probs * grad_probs, axis=-1, keepdims=True)
        grad_scores = (probs * centred * scale).astype(BF)
        grad_q_out[:, cols] = mm(grad_scores, k, NN).astype(BF)
        grad_kv[:, cols] = mm(grad_scores, q, TN).astype(BF)
        grad_kv[:, right] = mm(probs.astype(BF), g, TN).astype(BF)
    term = mm(grad_kv[...], w_ref[...], NT).astype(BF)
    term_out[...] = term.reshape(term_out.shape)


def attend(place, coded, w_kv, queries_grads, grad_q, pair_count):
    entries, length, width = coded.shape
    tokens, both = queries_grads.shape
    inner = both // 2
    stretches = entries // pair_count
    stretch_len = tokens // (4 * stretches)
    span = pair_count * length
    coded_spec = pl.BlockSpec((pair_count, length, width), lambda t, place: (t, 0, 0))
    at_place = lambda t, place: (place[0] * stretches + t, 0)
    in_specs = [
        coded_spec,
        pl.BlockSpec((width, both), lambda t, place: (0, 0)),
        pl.BlockSpec((stretch_len, both), at_place),
    ]
    operands = [coded, w_kv, queries_grads]
    aliases = {}
    if grad_q is not None:
        in_specs.append(pl.BlockSpec(memory_space=pl.ANY))
        operands.append(grad_q)
        aliases = {4: 1}
    return pl.pallas_call(
        attend_kernel,
        grid_spec=pltpu.PrefetchScalarGridSpec(
            num_scalar_prefetch=1,
            grid=(stretches,),
            in_specs=in_specs,
            out_specs=[coded_spec, pl.BlockSpec((stretch_len, inner), at_place)],
            scratch_shapes=[pltpu.VMEM((span, both), BF)] * 2,
        ),
        out_shape=[
            jax.ShapeDtypeStruct(coded.shape, BF),
            jax.ShapeDtypeStruct((tokens, inner), BF),
        ],
        input_output_aliases=aliases,
        compiler_params=pltpu.CompilerParams(vmem_limit_bytes=VMEM_LIMIT),
        cost_estimate=cost(
            4 * entries * length * width * both + 10 * stretches * stretch_len * span * inner,
            2 * (2 * entries * length * width + width * both + 3 * tokens * inner // 4),
        ),
        name="attend",
    )(place, *operands)


def grad_x_kernel(place_ref, q_ref, c_ref, w_ref, wc_ref, o_ref):
    shards, rows, width = w_ref.shape
    w = w_ref[...].reshape(shards * rows, width)
    o_ref[...] = (mm(q_ref[...], w, NT) + mm(c_ref[...], wc_ref[...], NT)).astype(BF)


def grad_x_block(place, grad_q, cond_sum, gathered, cond_full, rows, blocks):
    tokens, inner = grad_q.shape
    model, cond_width = cond_full.shape
    columns = model // blocks
    tiles = 2
    tile = columns // tiles
    return pl.pallas_call(
        grad_x_kernel,
        grid_spec=pltpu.PrefetchScalarGridSpec(
            num_scalar_prefetch=1,
            grid=(tiles,),
            in_specs=[
                pl.BlockSpec((tokens, inner), lambda i, place: (0, 0)),
                pl.BlockSpec((tokens, cond_width), lambda i, place: (0, 0)),
                pl.BlockSpec(
                    (tile // rows, rows, inner), lambda i, place: (place[0] * tiles + i, 0, 0)
                ),
                pl.BlockSpec((tile, cond_width), lambda i, place: (place[0] * tiles + i, 0)),
            ],
            out_specs=pl.BlockSpec((tokens, tile), lambda i, place: (0, i)),
        ),
        out_shape=jax.ShapeDtypeStruct((tokens, columns), BF),
        compiler_params=pltpu.CompilerParams(vmem_limit_bytes=VMEM_LIMIT),
        cost_estimate=cost(
            2 * tokens * columns * (inner + cond_width),
            2 * (tokens * (inner + cond_width + columns) + columns * (inner + cond_width)),
        ),
        name="grad_x_block",
    )(place, grad_q, cond_sum, gathered, cond_full)


def on_device(
    activations, grad_out, database, owners, row_index, w_cond, w_enc, w_query, w_kv, w_out
):
    stretches, pair_count = owners.shape
    tokens, model = activations.shape
    stretch_len = tokens // stretches
    db_rows, length, enc_width = database.shape
    ranks = lax.axis_size("ret")
    rank = lax.axis_index("ret")
    block = lax.axis_index("seq")
    home = stretches // ranks
    shard_rows, inner = w_query.shape
    cond_width = 2 * w_cond.shape[2]
    kv_rows = w_kv.shape[1]
    kv_pad = -kv_rows % 16

    cond_shard = jnp.transpose(w_cond, (1, 0, 2)).reshape(shard_rows, cond_width)
    cond_full = lax.all_gather(cond_shard, "seq", axis=0, tiled=True)
    kv_shard = jnp.pad(
        jnp.transpose(w_kv, (1, 0, 2)).reshape(kv_rows, 2 * inner), ((0, kv_pad), (0, 0))
    )
    packed = jnp.concatenate(
        [jnp.concatenate([w_query, w_out.T], axis=1), kv_shard], axis=0
    )
    gathered = lax.all_gather(packed, "seq", axis=0, tiled=False)
    kv_full = gathered[:, shard_rows : shard_rows + kv_rows].reshape(-1, 2 * inner)

    naming = jnp.stack([owners, row_index])
    naming = jnp.concatenate([along_seq(naming[:, -1:], 1), naming[:, :-1]], axis=1)
    owners_prev, rows_prev = naming[0], naming[1]
    tokens_prev = jnp.concatenate(
        [along_seq(activations[tokens - stretch_len :], 1), activations[: tokens - stretch_len]],
        axis=0,
    )
    last_row = jnp.sum(jnp.where(owners[-1] == rank, row_index[-1], 0))
    row_before = along_seq(lax.dynamic_slice_in_dim(database, last_row, 1, axis=0), 1)
    table = jnp.concatenate([database, row_before], axis=0)
    wanted = jnp.sum(jnp.where(owners_prev == rank, rows_prev, 0), axis=1)
    wanted = jnp.where(jnp.arange(stretches) == 0, db_rows, wanted)

    def rows_for(target):
        places = lax.dynamic_slice_in_dim(wanted, target * home, home)
        return jnp.take(table, places, axis=0)

    by_distance = [rows_for(rank)] + [
        around_ret(rows_for((rank + d) % ranks), d) for d in range(1, ranks)
    ]
    owners_home = lax.dynamic_slice_in_dim(owners_prev, rank * home, home)
    distance = (rank - owners_home) % ranks
    pick = (distance * home + jnp.arange(home)[:, None]).reshape(-1)
    rows_home = jnp.take(
        jnp.stack(by_distance).reshape(ranks * home, length, enc_width), pick, axis=0
    )
    entries = home * pair_count
    enc_queries = (
        mm(rows_home.reshape(entries * length, enc_width), w_enc[0], NN)
        .astype(BF)
        .reshape(rows_home.shape)
    )
    real = (block > 0) | (rank > 0) | (jnp.arange(entries) >= pair_count)
    keep = real.astype(jnp.int32)

    cond_part = mm(tokens_prev, cond_full, NN).astype(BF)
    home_tokens = home * stretch_len
    cond_home = lax.all_to_all(
        cond_part.reshape(ranks, home_tokens, cond_width), "ret", split_axis=0, concat_axis=0
    ).reshape(ranks, home_tokens, 2, cond_width // 2)
    cond_home = jnp.transpose(cond_home, (2, 1, 0, 3)).reshape(2, home_tokens, enc_width)
    cond_keys, cond_values = cond_home[0], cond_home[1]
    coded = encode(keep, rows_home, enc_queries, cond_keys, cond_values, w_enc[1], pair_count)

    queries_grads = projections(activations, grad_out, gathered, shard_rows)

    order = [0, 1, ranks - 1, 2]
    arrived = {d: (around_ret(coded, d) if d else coded) for d in order}
    grad_q, terms = None, {}
    for d in order:
        place = jnp.reshape((rank - d) % ranks, (1,)).astype(jnp.int32)
        term, grad_q = attend(place, arrived[d], kv_full, queries_grads, grad_q, pair_count)
        terms[d] = around_ret(term, -d) if d else term

    grad_wq = lax.psum_scatter(
        mm(activations, grad_q, TN).astype(BF), "seq", scatter_dimension=0, tiled=True
    )

    grad_rows, grad_keys, grad_values = encode_back(
        keep, [terms[d] for d in order], enc_queries, cond_keys, cond_values,
        w_enc[0], w_enc[1], pair_count,
    )

    cond_grad = jnp.stack([grad_keys, grad_values]).reshape(
        2, home_tokens, ranks, cond_width // 2
    )
    cond_grad = jnp.transpose(cond_grad, (2, 1, 0, 3)).reshape(ranks, home_tokens, cond_width)
    cond_sum = lax.all_to_all(cond_grad, "ret", split_axis=0, concat_axis=0).reshape(
        tokens, cond_width
    )
    cond_rows = lax.psum_scatter(
        mm(tokens_prev, cond_sum, TN).astype(BF), "seq", scatter_dimension=0, tiled=True
    )
    grad_wcond = jnp.transpose(cond_rows.reshape(shard_rows, 2, cond_width // 2), (1, 0, 2))
    cond_own = jnp.concatenate(
        [cond_sum[stretch_len:], along_seq(cond_sum[:stretch_len], -1)], axis=0
    )

    grad_rows = grad_rows.reshape(home, pair_count, length, enc_width)

    def rows_to(target):
        hits = (owners_home == target)[:, :, None, None]
        return jnp.sum(jnp.where(hits, grad_rows, jnp.zeros((), BF)).astype(F32), axis=1).astype(BF)

    returned = [rows_to(rank)] + [
        around_ret(rows_to((rank + d) % ranks), d) for d in range(1, ranks)
    ]

    def share(d):
        place = jnp.reshape((rank + d) % ranks, (1,)).astype(jnp.int32)
        return grad_x_block(place, grad_q, cond_own, gathered, cond_full, shard_rows, ranks)

    shares = [around_ret(share(d), d) for d in (2, 1, ranks - 1)] + [share(0)]
    grad_x = sum(part.astype(F32) for part in shares).astype(BF)

    returned = jnp.stack(returned)
    back_order = (rank - jnp.arange(ranks)) % ranks
    returned = jnp.take(returned, back_order, axis=0).reshape(stretches, length, enc_width)
    row_after = along_seq(returned[:1], -1)
    returned = jnp.concatenate([returned[1:], row_after], axis=0)
    mine = jnp.sum(jnp.where(owners == rank, row_index, 0), axis=1)
    named = jnp.any(owners == rank, axis=1)
    hits = (jnp.arange(db_rows)[:, None] == mine[None, :]) & named[None, :]
    grad_db = jnp.einsum(
        "rm,mle->rle", hits.astype(BF), returned, preferred_element_type=F32
    ).astype(BF)
    return (grad_x, grad_db, grad_wq, grad_wcond)


def solution(mesh):
    return jax.shard_map(
        on_device,
        mesh=mesh,
        in_specs=(
            P("seq", None),
            P("seq", None),
            P(("seq", "ret"), None, None),
            P("seq", None),
            P("seq", None),
            P(None, "seq", "ret"),
            P(),
            P("seq", "ret"),
            P(None, "seq", "ret"),
            P("ret", "seq"),
        ),
        out_specs=(
            P("seq", "ret"),
            P(("seq", "ret"), None, None),
            P("seq", "ret"),
            P(None, "seq", "ret"),
        ),
        check_vma=False,
    )
```
